32 devices in a mesh: wide: 8 (over y, x, core), narrow: 4 (over z).
Axes of the slice: x: 2, y: 2, z: 4, core: 2. Of those that a mesh axis runs over, the one named last changes fastest.
Arguments:
- heads_output: bfloat16 [512, 8192], P('narrow', 'wide'), may hold values from -6 to 6
- residual_in: bfloat16 [512, 16384], P('wide', 'narrow'), may hold values from -6 to 6
- out_weight: bfloat16 [8192, 16384], P('wide', 'narrow'), may hold values from -0.0625 to 0.0625
- norm_gain: float32 [16384], P('narrow'), may hold values from 0.1 to 1.9
- gate_weight: bfloat16 [16384, 26624], P('narrow', 'wide'), may hold values from -0.046875 to 0.046875
- up_weight: bfloat16 [16384, 26624], P('narrow', 'wide'), may hold values from -0.046875 to 0.046875
Outputs:
- residual: float32 [512, 16384], P('wide', 'narrow')
- hidden: float32 [512, 26624], P('narrow', 'wide')
The draws below stay inside these ranges and needn't reach their ends.
All inputs are finite; a program needn't handle non-finite values.
Results may differ from the reference program's by a relative error of at most 0.0041.
Values may be sent and summed in bfloat16 or wider, within the bound.
No kernel may reach another device: no remote copies, remote signals or barrier semaphores. Data moves between devices by JAX's collectives and lax.ppermute only.
A program may use at most 128 MiB of HBM per device.

```python
import jax
import jax.numpy as jnp
from jax import lax

D = 16384
FF = 26624
HEADS = 64
HEAD_DIM = 128
TOKENS = 512


def spiked(values, rng, source, target, shards_of, factor):
    owner, partner = [(jnp.arange(values.shape[dim]) // (values.shape[dim] // shards_of)).reshape([-1 if axis == dim else 1 for axis in range(values.ndim)]) for dim in (source, target)]
    chosen = jax.random.permutation(rng, shards_of)[partner]
    strong = (owner == chosen) | (owner == (partner + shards_of // 2) % shards_of)
    return jnp.where(strong, factor * values, values)


def levels(rng, shape, cuts, smallest, largest):
    factor_of, own = 1.0, jax.random.fold_in(rng, 6)
    for axis_at, parts in cuts:
        steps = jnp.exp(jax.random.uniform(jax.random.fold_in(own, axis_at), (parts,), jnp.float32, smallest / len(cuts), largest / len(cuts)))
        factor_of = factor_of * jnp.repeat(steps, shape[axis_at] // parts).reshape([-1 if axis == axis_at else 1 for axis in range(len(shape))])
    return factor_of


def normal_values(key, dims, spread, most, cuts=(), dtype=jnp.bfloat16):
    loudness = levels(key, dims, cuts, -0.22, 0.18) if cuts else 1.0
    array = jax.random.normal(key, dims, jnp.float32) * spread * loudness
    return jnp.minimum(jnp.maximum(array, -most), most).astype(dtype)


def heavy_noise(own_key, extent, scale, reach, shards, heavy, held_as=jnp.bfloat16):
    values = scale * jax.random.normal(own_key, extent, jnp.float32)
    if shards:
        values = values * levels(own_key, extent, shards, -0.22, 0.18)
    return jnp.clip(spiked(values, jax.random.fold_in(own_key, 3), *heavy), -reach, reach).astype(held_as)


def setup_inputs(seed: int = 0) -> dict:
    splits = jax.random.split(jax.random.key(seed), 7)
    return {
        "heads_output": heavy_noise(splits[0], (TOKENS, HEADS * HEAD_DIM), 1.0, 6.0, ((0, 4), (1, 8)), (1, 0, 8, 2.0)),
        "residual_in": normal_values(splits[1], (TOKENS, D), 1.0, 6.0, ((0, 8), (1, 4))),
        "out_weight": normal_values(splits[2], (HEADS * HEAD_DIM, D), (HEADS * HEAD_DIM) ** -0.5, 0.0625, ((0, 8), (1, 4))),
        "norm_gain": jnp.clip(1.0 + 0.18 * jax.random.normal(splits[3], (D,), jnp.float32), 0.1, 1.9),
        "gate_weight": normal_values(splits[4], (D, FF), D ** -0.5, 0.046875, ((0, 4), (1, 8))),
        "up_weight": normal_values(splits[5], (D, FF), D ** -0.5, 0.046875, ((0, 4), (1, 8))),
    }


def reference(heads_output, residual_in, out_weight, norm_gain, gate_weight, up_weight):
    attended = jnp.dot(heads_output, out_weight, preferred_element_type=jnp.float32)
    residual = residual_in.astype(jnp.float32) + attended
    squares = lax.optimization_barrier(jnp.sum(residual * residual, axis=1))
    scale = 1.0 / jnp.sqrt(squares / D + 1e-05)
    normed = (residual * scale[:, None] * norm_gain).astype(jnp.bfloat16)
    gate = jnp.dot(normed, gate_weight, preferred_element_type=jnp.float32)
    up = jnp.dot(normed, up_weight, preferred_element_type=jnp.float32)
    hidden = jax.nn.silu(gate) * up
    return (residual, hidden)
```

```python
import jax
import jax.numpy as jnp
from jax import lax
from jax.sharding import PartitionSpec as P

F32, BF16 = jnp.float32, jnp.bfloat16
SHARES = (32, 32)


def pick(value, index, axis=0):
    return lax.dynamic_index_in_dim(value, index, axis, keepdims=False)


def tie(value, after):
    return lax.optimization_barrier((value, after))[0] if after else value


def solution(mesh):
    wide, narrow = mesh.shape["wide"], mesh.shape["narrow"]
    chips = wide // 2
    assert chips == narrow

    def swap(value, bits):
        return lax.ppermute(value, "wide", [(i, i ^ bits) for i in range(wide)])

    def shift(value, by):
        return lax.ppermute(value, "narrow", [(i, (i + by) % narrow) for i in range(narrow)])

    def hop(value, step):
        pairs = [(step - 1, step), (narrow - step, narrow - 1 - step)]
        return lax.ppermute(value, "narrow", pairs)

    def on_device(heads_output, residual_in, out_weight, norm_gain, gate_weight, up_weight):
        me, place = lax.axis_index("wide"), lax.axis_index("narrow")
        chip, core = me // 2, me % 2
        rows, width = residual_in.shape
        features = width * narrow
        depth = heads_output.shape[1]
        heads = heads_output.reshape(2, rows, depth)

        def fetch(at, share, after):
            own = tie(heads[:, at : at + share], after)
            return jnp.stack([own] + [shift(own, s) for s in range(1, narrow)])

        def project(stacked):
            share = stacked.shape[2]

            def terms(which):
                left = pick(stacked, which, 1).reshape(narrow * share, depth)
                return jnp.dot(left, out_weight, preferred_element_type=F32)

            sent = terms(1 - core)
            got = swap(sent, 1)
            kept, _ = lax.optimization_barrier((terms(core), sent))
            return kept, got

        def spread(kept, got):
            total = (kept + got).reshape(narrow, -1, width)

            def for_chip(d):
                return pick(total, (place - (chip ^ d)) % narrow)

            return for_chip(0), [swap(for_chip(d), 2 * d) for d in range(1, chips)]

        def scale_of(residual, after):
            own = jnp.sum(residual * residual, axis=1)
            others = tie([shift(own, s) for s in range(1, narrow)], after)
            return 1.0 / jnp.sqrt(sum(others, own) / features + 1e-05)

        def gather(normed, after):
            return jnp.stack([normed] + tie([swap(normed, 2 * d) for d in range(1, chips)], after))

        def both(near):
            near = jnp.stack([pick(near, j ^ chip) for j in range(chips)])
            return jnp.stack([near, swap(near, 1)], 1)

        def multiply(all_rows, weight, after):
            left = tie(all_rows.reshape(-1, width), after)
            terms = jnp.dot(left, weight, preferred_element_type=F32)
            return terms.reshape(*all_rows.shape[:-1], -1)

        def reduce_call(terms):
            return lax.psum_scatter(terms.astype(BF16), "narrow", scatter_dimension=0, tiled=True)

        def staged_sums(gate, up, beside):
            terms = (gate, up)
            far = narrow - 1
            items = [(0, far)]
            for b in range(far - 1, -1, -1):
                items += ([(0, b)] if b else []) + [(1, b + 1)]
            waiting = [items[:1]] + [items[i : i + 2] for i in range(1, len(items), 2)]
            totals = [pick(t, place) for t in terms]
            flying, stage = [], 0
            while waiting or flying:
                entering = waiting.pop(0) if waiting else []
                lanes = {}
                for which, b, step, carried in flying + [(which, b, 0, 0.0) for which, b in entering]:
                    index = jnp.where(place == step, b, narrow - 1 - b)
                    part = (pick(terms[which], index) + carried).astype(BF16)
                    lanes.setdefault(step + 1, []).append((which, b, part))
                moved = {step: hop(jnp.stack([part for _, _, part in lane]), step) for step, lane in lanes.items()}
                moved, _ = lax.optimization_barrier((moved, beside[stage] if stage < len(beside) else ()))
                stage += 1
                flying = []
                for step, lane in lanes.items():
                    for (which, b, _), value in zip(lane, moved[step]):
                        if step == b:
                            totals[which] = totals[which] + value
                        else:
                            flying.append((which, b, step, value))
            return totals

        first, second = SHARES
        stacked_a = fetch(0, first, ())
        kept_a, got_a = project(stacked_a)
        whole = lax.all_gather(tie(heads, (stacked_a,)), "narrow", axis=0)
        own_a, parts_a = spread(kept_a, got_a)
        stacked_b = jnp.stack([pick(whole, (place - s) % narrow) for s in range(narrow)])[:, :, first:]
        residual_a = residual_in[:first].astype(F32) + sum(parts_a, own_a)
        scale_a = scale_of(residual_a, ())
        normed_a = (residual_a * scale_a[:, None] * norm_gain).astype(BF16)
        kept_b, got_b = project(tie(stacked_b, (normed_a,)))
        near_a = gather(normed_a, (kept_b,))
        rows_a = both(near_a)

        own_b, parts_b = spread(tie(kept_b, (near_a,)), got_b)
        gate_a = multiply(rows_a, gate_weight, ())
        gate_sum_a = reduce_call(gate_a)
        parts_b = tie(parts_b, (gate_a,))
        residual_b = residual_in[first:].astype(F32) + sum(parts_b, own_b)
        scale_b = scale_of(residual_b, ())
        normed_b = (residual_b * scale_b[:, None] * norm_gain).astype(BF16)
        up_a = multiply(rows_a, up_weight, (gate_a, normed_b))
        up_sum_a = reduce_call(up_a)
        rows_b = both(gather(normed_b, (up_a,)))
        gate_b = multiply(rows_b, gate_weight, (gate_sum_a,))
        up_b = multiply(rows_b, up_weight, (gate_b,))
        gate_sum_b, up_sum_b = staged_sums(gate_b, up_b, ((up_b,), (up_sum_a,)))

        residuals = [residual_a, residual_b]
        outs = []
        for gate, up in ((gate_sum_a[0], up_sum_a[0]), (gate_sum_b, up_sum_b)):
            hidden = jax.nn.silu(gate.astype(F32)) * up.astype(F32)
            outs.append(jnp.where(core == 0, hidden, hidden[::-1]))
        hidden = jnp.concatenate(outs, axis=1)
        return jnp.concatenate(residuals, axis=0), hidden.reshape(2 * rows, -1)

    in_specs = (
        P("narrow", "wide"),
        P("wide", "narrow"),
        P("wide", "narrow"),
        P("narrow"),
        P("narrow", "wide"),
        P("narrow", "wide"),
    )
    out_specs = (P("wide", "narrow"), P("narrow", "wide"))
    return jax.shard_map(on_device, mesh=mesh, in_specs=in_specs, out_specs=out_specs, check_vma=False)
```

```python
import jax
import jax.numpy as jnp
from jax import lax
from jax.sharding import PartitionSpec as P

F32, BF16 = jnp.float32, jnp.bfloat16
SHARES = (32, 32)


def pick(value, index, axis=0):
    return lax.dynamic_index_in_dim(value, index, axis, keepdims=False)


def tie(value, after):
    return lax.optimization_barrier((value, after))[0] if after else value


def solution(mesh):
    wide, narrow = mesh.shape["wide"], mesh.shape["narrow"]
    chips = wide // 2
    assert chips == narrow

    def swap(value, bits):
        return lax.ppermute(value, "wide", [(i, i ^ bits) for i in range(wide)])

    def shift(value, by):
        return lax.ppermute(value, "narrow", [(i, (i + by) % narrow) for i in range(narrow)])

    def hop(value, step):
        pairs = [(step - 1, step), (narrow - step, narrow - 1 - step)]
        return lax.ppermute(value, "narrow", pairs)

    def on_device(heads_output, residual_in, out_weight, norm_gain, gate_weight, up_weight):
        me, place = lax.axis_index("wide"), lax.axis_index("narrow")
        chip, core = me // 2, me % 2
        rows, width = residual_in.shape
        features = width * narrow
        depth = heads_output.shape[1]
        heads = heads_output.reshape(2, rows, depth)

        def fetch(at, share, after):
            own = tie(heads[:, at : at + share], after)
            return jnp.stack([own] + [shift(own, s) for s in range(1, narrow)])

        def project(stacked):
            share = stacked.shape[2]

            def terms(which):
                left = pick(stacked, which, 1).reshape(narrow * share, depth)
                return jnp.dot(left, out_weight, preferred_element_type=F32)

            sent = terms(1 - core)
            got = swap(sent, 1)
            kept, _ = lax.optimization_barrier((terms(core), sent))
            return kept, got

        def spread(kept, got, travel):
            total = (kept + got).reshape(narrow, -1, width)

            def for_chip(d):
                return pick(total, (place - (chip ^ d)) % narrow)

            sent = [for_chip(d).astype(travel) for d in range(1, chips)]
            return for_chip(0), sent, [swap(part, 2 * d) for d, part in enumerate(sent, 1)]

        def scale_of(residual, after):
            own = jnp.sum(residual * residual, axis=1)
            others = tie([shift(own, s) for s in range(1, narrow)], after)
            return 1.0 / jnp.sqrt(sum(others, own) / features + 1e-05)

        def gather(normed, after):
            return jnp.stack([normed] + tie([swap(normed, 2 * d) for d in range(1, chips)], after))

        def both(near):
            near = jnp.stack([pick(near, j ^ chip) for j in range(chips)])
            return jnp.stack([near, swap(near, 1)], 1)

        def multiply(all_rows, weight, after):
            left = tie(all_rows.reshape(-1, width), after)
            terms = jnp.dot(left, weight, preferred_element_type=F32)
            return terms.reshape(*all_rows.shape[:-1], -1)

        totals, flying, last = {}, [], ()

        def stage(entering, beside=None, after=()):
            nonlocal flying, last
            lanes = {}
            for terms, b in entering:
                totals.setdefault(id(terms), pick(terms, place))
            for terms, b, step, carried in flying + [(terms, b, 0, 0.0) for terms, b in entering]:
                index = jnp.where(place == step, b, narrow - 1 - b)
                part = (pick(terms, index) + carried).astype(BF16)
                lanes.setdefault(step + 1, []).append((terms, b, part))
            parts = {step: jnp.stack([part for _, _, part in lane]) for step, lane in lanes.items()}
            parts, _ = lax.optimization_barrier((parts, (last, after)))
            moved = {step: hop(part, step) for step, part in parts.items()}
            last = tuple(moved.values())
            product = beside(tuple(parts.values())) if beside else ()
            moved, _ = lax.optimization_barrier((moved, product))
            flying = []
            for step, lane in lanes.items():
                for (terms, b, _), value in zip(lane, moved[step]):
                    if step == b:
                        totals[id(terms)] = totals[id(terms)] + value
                    else:
                        flying.append((terms, b, step, value))
            return product

        first, second = SHARES
        far = narrow - 1
        stacked_a = fetch(0, first, ())
        kept_a, got_a = project(stacked_a)
        stacked_b = fetch(first, second, (stacked_a,))
        own_a, _, parts_a = spread(kept_a, got_a, BF16)
        parts_a = tie(parts_a, (stacked_b,))
        residual_a = residual_in[:first].astype(F32) + sum(parts_a, own_a)
        scale_a = scale_of(residual_a, ())
        normed_a = (residual_a * scale_a[:, None] * norm_gain).astype(BF16)
        kept_b, got_b = project(tie(stacked_b, (normed_a,)))
        near_a = gather(normed_a, (kept_b,))
        rows_a = both(near_a)

        own_b, sent_b, parts_b = spread(tie(kept_b, (near_a,)), got_b, F32)
        gate_a = multiply(rows_a, gate_weight, (sent_b,))
        up_a = stage(
            [(gate_a, b) for b in range(far, 1, -1)],
            lambda sent: multiply(rows_a, up_weight, (gate_a, sent)),
        )
        residual_b = residual_in[first:].astype(F32) + sum(tie(parts_b, (up_a,)), own_b)
        scale_b = scale_of(residual_b, ())
        normed_b = (residual_b * scale_b[:, None] * norm_gain).astype(BF16)
        rows_b = both(
            stage(
                [(gate_a, 1), (up_a, far)],
                lambda sent: gather(tie(normed_b, (sent,)), ()),
                (normed_b,),
            )
        )
        before = last

        def products(sent):
            gate = multiply(rows_b, gate_weight, (before, sent))
            return gate, multiply(rows_b, up_weight, (gate,))

        gate_b, up_b = stage([(up_a, b) for b in range(far - 1, 0, -1)], products)
        for b in range(far, 0, -1):
            stage([(gate_b, b), (up_b, b)])
        while flying:
            stage([])
        gate_sum_a, up_sum_a, gate_sum_b, up_sum_b = (totals[id(t)] for t in (gate_a, up_a, gate_b, up_b))

        residuals = [residual_a, residual_b]
        outs = []
        for gate, up in ((gate_sum_a, up_sum_a), (gate_sum_b, up_sum_b)):
            hidden = jax.nn.silu(gate) * up
            outs.append(jnp.where(core == 0, hidden, hidden[::-1]))
        hidden = jnp.concatenate(outs, axis=1)
        return jnp.concatenate(residuals, axis=0), hidden.reshape(2 * rows, -1)

    in_specs = (
        P("narrow", "wide"),
        P("wide", "narrow"),
        P("wide", "narrow"),
        P("narrow"),
        P("narrow", "wide"),
        P("narrow", "wide"),
    )
    out_specs = (P("wide", "narrow"), P("narrow", "wide"))
    return jax.shard_map(on_device, mesh=mesh, in_specs=in_specs, out_specs=out_specs, check_vma=False)
```

```python
import jax
import jax.numpy as jnp
from jax import lax
from jax.sharding import PartitionSpec as P

F32, BF16 = jnp.float32, jnp.bfloat16
SHARES = (32, 32)


def pick(value, index, axis=0):
    return lax.dynamic_index_in_dim(value, index, axis, keepdims=False)


def tie(value, after):
    return lax.optimization_barrier((value, after))[0] if after else value


def solution(mesh):
    wide, narrow = mesh.shape["wide"], mesh.shape["narrow"]
    chips = wide // 2
    assert chips == narrow

    def swap(value, bits):
        return lax.ppermute(value, "wide", [(i, i ^ bits) for i in range(wide)])

    def shift(value, by):
        return lax.ppermute(value, "narrow", [(i, (i + by) % narrow) for i in range(narrow)])

    def hop(value, step):
        pairs = [(step - 1, step), (narrow - step, narrow - 1 - step)]
        return lax.ppermute(value, "narrow", pairs)

    def on_device(heads_output, residual_in, out_weight, norm_gain, gate_weight, up_weight):
        me, place = lax.axis_index("wide"), lax.axis_index("narrow")
        chip, core = me // 2, me % 2
        rows, width = residual_in.shape
        features = width * narrow
        depth = heads_output.shape[1]
        heads = heads_output.reshape(2, rows, depth)

        def fetch(at, share, after):
            own = tie(heads[:, at : at + share], after)
            return jnp.stack([own] + [shift(own, s) for s in range(1, narrow)])

        def project(stacked):
            share = stacked.shape[2]

            def terms(which):
                left = pick(stacked, which, 1).reshape(narrow * share, depth)
                return jnp.dot(left, out_weight, preferred_element_type=F32)

            sent = terms(1 - core)
            got = swap(sent, 1)
            kept, _ = lax.optimization_barrier((terms(core), sent))
            return kept, got

        def spread(kept, got, travel):
            total = (kept + got).reshape(narrow, -1, width)

            def for_chip(d):
                return pick(total, (place - (chip ^ d)) % narrow)

            sent = [for_chip(d).astype(travel) for d in range(1, chips)]
            return for_chip(0), sent, [swap(part, 2 * d) for d, part in enumerate(sent, 1)]

        def scale_of(residual, after):
            own = jnp.sum(residual * residual, axis=1)
            others = tie([shift(own, s) for s in range(1, narrow)], after)
            return 1.0 / jnp.sqrt(sum(others, own) / features + 1e-05)

        def gather(normed, after):
            return jnp.stack([normed] + tie([swap(normed, 2 * d) for d in range(1, chips)], after))

        def both(near):
            near = jnp.stack([pick(near, j ^ chip) for j in range(chips)])
            return jnp.stack([near, swap(near, 1)], 1)

        def multiply(all_rows, weight, after):
            left = tie(all_rows.reshape(-1, width), after)
            terms = jnp.dot(left, weight, preferred_element_type=F32)
            return terms.reshape(*all_rows.shape[:-1], -1)

        totals, flying, last = {}, [], ()

        def stage(entering, beside=None, after=()):
            nonlocal flying, last
            lanes = {}
            for terms, b in entering:
                totals.setdefault(id(terms), pick(terms, place))
            for terms, b, step, carried in flying + [(terms, b, 0, 0.0) for terms, b in entering]:
                index = jnp.where(place == step, b, narrow - 1 - b)
                part = (pick(terms, index) + carried).astype(BF16)
                lanes.setdefault(step + 1, []).append((terms, b, part))
            parts = {step: jnp.stack([part for _, _, part in lane]) for step, lane in lanes.items()}
            parts, _ = lax.optimization_barrier((parts, (last, after)))
            moved = {step: hop(part, step) for step, part in parts.items()}
            last = tuple(moved.values())
            product = beside(tuple(parts.values())) if beside else ()
            moved, _ = lax.optimization_barrier((moved, product))
            flying = []
            for step, lane in lanes.items():
                for (terms, b, _), value in zip(lane, moved[step]):
                    if step == b:
                        totals[id(terms)] = totals[id(terms)] + value
                    else:
                        flying.append((terms, b, step, value))
            return product

        first, second = SHARES
        far = narrow - 1
        stacked_a = fetch(0, first, ())
        kept_a, got_a = project(stacked_a)
        stacked_b = fetch(first, second, (stacked_a,))
        own_a, _, parts_a = spread(kept_a, got_a, BF16)
        parts_a = tie(parts_a, (stacked_b,))
        residual_a = residual_in[:first].astype(F32) + sum(parts_a, own_a)
        scale_a = scale_of(residual_a, ())
        normed_a = (residual_a * scale_a[:, None] * norm_gain).astype(BF16)
        kept_b, got_b = project(tie(stacked_b, (normed_a,)))
        near_a = gather(normed_a, (kept_b,))
        rows_a = both(near_a)

        own_b, sent_b, parts_b = spread(tie(kept_b, (near_a,)), got_b, F32)
        gate_a = multiply(rows_a, gate_weight, (sent_b,))
        up_a = stage(
            [(gate_a, b) for b in range(far, 1, -1)],
            lambda sent: multiply(rows_a, up_weight, (gate_a, sent)),
        )
        residual_b = residual_in[first:].astype(F32) + sum(tie(parts_b, (up_a,)), own_b)
        scale_b = scale_of(residual_b, ())
        normed_b = (residual_b * scale_b[:, None] * norm_gain).astype(BF16)
        rows_b = both(
            stage(
                [(gate_a, 1), (up_a, far)],
                lambda sent: gather(tie(normed_b, (sent,)), ()),
                (normed_b,),
            )
        )
        before = last

        def products(sent):
            gate = multiply(rows_b, gate_weight, (before, sent))
            return gate, multiply(rows_b, up_weight, (gate,))

        gate_b, up_b = stage([(up_a, b) for b in range(far - 1, 0, -1)], products)
        for b in range(far, 0, -1):
            stage([(gate_b, b), (up_b, b)])
        while flying:
            stage([])
        gate_sum_a, up_sum_a, gate_sum_b, up_sum_b = (totals[id(t)] for t in (gate_a, up_a, gate_b, up_b))

        hidden = jnp.zeros((2, rows, gate_weight.shape[1]), F32)
        for at, gate, up in ((0, gate_sum_a, up_sum_a), (first, gate_sum_b, up_sum_b)):
            part = jax.nn.silu(gate) * up
            part = jnp.where(core == 0, part, part[::-1])
            hidden = lax.optimization_barrier(lax.dynamic_update_slice_in_dim(hidden, part, at, 1))
        residual = jnp.concatenate([residual_a, residual_b], axis=0)
        return residual, hidden.reshape(2 * rows, -1)

    in_specs = (
        P("narrow", "wide"),
        P("wide", "narrow"),
        P("wide", "narrow"),
        P("narrow"),
        P("narrow", "wide"),
        P("narrow", "wide"),
    )
    out_specs = (P("wide", "narrow"), P("narrow", "wide"))
    return jax.shard_map(on_device, mesh=mesh, in_specs=in_specs, out_specs=out_specs, check_vma=False)
```
